32 devices in a mesh: row: 8 (over y, x, core), col: 4 (over z).
Axes of the slice: x: 2, y: 2, z: 4, core: 2. Of those that a mesh axis runs over, the one named last changes fastest.
Arguments:
- activations: bfloat16 [128, 8192], P('row', 'col'), may hold values from -6 to 6
- out_grad: bfloat16 [128, 8192], P('row', 'col'), may hold values from -1.5 to 1.5
- w_gate: bfloat16 [8192, 14336], P('col', 'row'), may hold values from -0.0625 to 0.0625
- w_up: bfloat16 [8192, 14336], P('col', 'row'), may hold values from -0.0625 to 0.0625
- w_down: bfloat16 [14336, 8192], P('row', 'col'), may hold values from -0.046875 to 0.046875
Outputs:
- in_grad: bfloat16 [128, 8192], P('row', 'col')
- grad_gate: bfloat16 [8192, 14336], P('col', 'row')
- grad_up: bfloat16 [8192, 14336], P('col', 'row')
- grad_down: bfloat16 [14336, 8192], P('row', 'col')
The draws below stay inside these ranges and needn't reach their ends.
All inputs are finite; a program needn't handle non-finite values.
Results may differ from the reference program's by a relative error of at most 0.0049.
Values may be sent and summed in bfloat16 or wider, within the bound.
A program may use at most 128 MiB of HBM per device.

```python
import jax
import jax.numpy as jnp
from jax import lax

D = 8192
FF = 14336
TOKENS = 128


def raised(array, own_key, source, target, shards_of, factor):
    def block_of(axis_at):
        return (jnp.arange(array.shape[axis_at]) // (array.shape[axis_at] // shards_of)).reshape((-1,) + (1,) * (array.ndim - 1 - axis_at))

    one_side = jax.random.permutation(own_key, shards_of)[block_of(target)]
    other_side = (block_of(target) + shards_of // 2) % shards_of
    return jnp.where((block_of(source) == one_side) | (block_of(source) == other_side), factor * array, array)


def block_scale(own_key, dims, cuts, smallest, largest):
    factor_of = 1.0
    for dim, parts in cuts:
        heights = jax.random.uniform(jax.random.fold_in(jax.random.fold_in(own_key, 6), dim), (parts,), jnp.float32, smallest / len(cuts), largest / len(cuts))
        factor_of = factor_of * jnp.repeat(jnp.exp(heights), dims[dim] // parts).reshape((-1,) + (1,) * (len(dims) - 1 - dim))
    return factor_of


def gaussian(rng, dims, width, reach, pieces=(), kind=jnp.bfloat16):
    drawn = width * jax.random.normal(rng, dims, jnp.float32)
    if pieces:
        drawn = drawn * block_scale(rng, dims, pieces, -0.22, 0.18)
    return jnp.clip(drawn, -reach, reach).astype(kind)


def noise_with(rng, dims, scale, reach, cuts, heavy, kind=jnp.bfloat16):
    array = scale * jax.random.normal(rng, dims, jnp.float32)
    if cuts:
        array = array * block_scale(rng, dims, cuts, -0.22, 0.18)
    return jnp.clip(raised(array, jax.random.fold_in(rng, 3), *heavy), -reach, reach).astype(kind)


def setup_inputs(seed: int = 0) -> dict:
    splits = jax.random.split(jax.random.key(seed), 6)
    return {
        "activations": noise_with(splits[0], (TOKENS, D), 1.0, 6.0, ((0, 8), (1, 4)), (1, 0, 8, 2.0)),
        "out_grad": noise_with(splits[1], (TOKENS, D), 0.25, 1.5, ((0, 8), (1, 4)), (1, 0, 8, 2.0)),
        "w_gate": gaussian(splits[2], (D, FF), D ** -0.5, 0.0625, ((0, 4), (1, 8))),
        "w_up": gaussian(splits[3], (D, FF), D ** -0.5, 0.0625, ((0, 4), (1, 8))),
        "w_down": gaussian(splits[4], (FF, D), FF ** -0.5, 0.046875, ((0, 8), (1, 4))),
    }


def reference(activations, out_grad, w_gate, w_up, w_down):
    contract_last = (((1,), (1,)), ((), ()))
    gate = jnp.dot(activations, w_gate, preferred_element_type=jnp.float32)
    up_val = jnp.dot(activations, w_up, preferred_element_type=jnp.float32)
    hidden_grad = lax.dot_general(out_grad, w_down, contract_last, preferred_element_type=jnp.float32)
    sigma = jax.nn.sigmoid(gate)
    hidden = (gate * sigma * up_val).astype(jnp.bfloat16)
    up_grad = (hidden_grad * gate * sigma).astype(jnp.bfloat16)
    gate_grad = (hidden_grad * up_val * sigma * (1.0 + gate * (1.0 - sigma))).astype(jnp.bfloat16)
    grad_down = jnp.dot(hidden.T, out_grad, preferred_element_type=jnp.float32).astype(jnp.bfloat16)
    grad_gate = jnp.dot(activations.T, gate_grad, preferred_element_type=jnp.float32).astype(jnp.bfloat16)
    grad_up = jnp.dot(activations.T, up_grad, preferred_element_type=jnp.float32).astype(jnp.bfloat16)
    in_sum = lax.dot_general(gate_grad, w_gate, contract_last, preferred_element_type=jnp.float32)
    in_sum = in_sum + lax.dot_general(up_grad, w_up, contract_last, preferred_element_type=jnp.float32)
    return in_sum.astype(jnp.bfloat16), grad_gate, grad_up, grad_down
```

```python
import functools

import jax
import jax.numpy as jnp
from jax import lax
from jax.experimental import pallas as pl
from jax.experimental.pallas import tpu as pltpu
from jax.sharding import PartitionSpec as P


def swiglu_parts(summed, width):
    gate = summed[:, :width]
    up_val = summed[:, width : 2 * width]
    hidden_grad = summed[:, 2 * width :]
    sigma = jax.nn.sigmoid(gate)
    hidden = (gate * sigma * up_val).astype(jnp.bfloat16)
    up_grad = (hidden_grad * gate * sigma).astype(jnp.bfloat16)
    gate_grad = (hidden_grad * up_val * sigma * (1.0 + gate * (1.0 - sigma))).astype(jnp.bfloat16)
    return (hidden, gate_grad, up_grad)


def on_device(activations, out_grad, w_gate, w_up, w_down):
    inputs, grads = (
        lax.all_gather(activations, "row", axis=0, tiled=True),
        lax.all_gather(out_grad, "row", axis=0, tiled=True),
    )
    width = w_gate.shape[1]
    contract_last = (((1,), (1,)), ((), ()))
    contract_first = (((0,), (0,)), ((), ()))
    gate_part = jnp.dot(inputs, w_gate, preferred_element_type=jnp.float32)
    up_part = jnp.dot(inputs, w_up, preferred_element_type=jnp.float32)
    back_part = lax.dot_general(grads, w_down, contract_last, preferred_element_type=jnp.float32)
    summed = lax.psum(jnp.concatenate([gate_part, up_part, back_part], axis=1), "col")
    hidden, gate_grad, up_grad = swiglu_parts(summed, width)
    grad_down = lax.dot_general(
        hidden, grads, contract_first, preferred_element_type=jnp.float32
    ).astype(jnp.bfloat16)
    grad_gate = lax.dot_general(
        inputs, gate_grad, contract_first, preferred_element_type=jnp.float32
    ).astype(jnp.bfloat16)
    grad_up = lax.dot_general(
        inputs, up_grad, contract_first, preferred_element_type=jnp.float32
    ).astype(jnp.bfloat16)
    term = lax.dot_general(gate_grad, w_gate, contract_last, preferred_element_type=jnp.float32)
    in_grad = lax.psum_scatter(
        term + lax.dot_general(up_grad, w_up, contract_last, preferred_element_type=jnp.float32),
        "row",
        scatter_dimension=0,
        tiled=True,
    ).astype(jnp.bfloat16)
    return (in_grad, grad_gate, grad_up, grad_down)


MESH = pl.DeviceIdType.MESH
CHUNK = 256


def nt_dot(a, b):
    return lax.dot_general(a, b, (((1,), (1,)), ((), ())), preferred_element_type=jnp.float32)


def tn_dot(a, b):
    return lax.dot_general(a, b, (((0,), (0,)), ((), ())), preferred_element_type=jnp.float32)


def exchange_kernel(
    act_ref, grad_ref, wg_ref, wu_ref, wd_ref,
    in_grad_ref, act_out, grad_out, hidden_out, gate_out, up_out,
    both, wgu, wdn, ep, rp, xp, res, own, acc, pair, send_buf, recv_buf,
    w_sem, gat_send, gat_recv, ep_send, rp_recv, xp_send, xp_recv, res_send, res_recv,
    pair_send, pair_recv, rs_send, rs_recv, own_sem,
):
    chunks = wgu.shape[0]
    rows, width = act_ref.shape
    half = rows * 4
    r = lax.axis_index("row")
    c = lax.axis_index("col")
    core = lax.rem(r, 2)
    x = lax.rem(r // 2, 2)
    y = r // 4
    sib = r + 1 - 2 * core
    xn = r + 2 - 4 * x
    yn = r + 4 - 8 * y
    dg = xn + 4 - 8 * y
    last = chunks - 1

    def weight_copies(j):
        cols = pl.ds(pl.multiple_of(j * CHUNK, CHUNK), CHUNK)
        return (
            pltpu.make_async_copy(wg_ref.at[:, cols], wgu.at[j, :, pl.ds(0, CHUNK)], w_sem.at[0, j]),
            pltpu.make_async_copy(wu_ref.at[:, cols], wgu.at[j, :, pl.ds(CHUNK, CHUNK)], w_sem.at[1, j]),
            pltpu.make_async_copy(wd_ref.at[cols, :], wdn.at[j], w_sem.at[2, j]),
        )

    def start_weights(j, carry):
        for copy in weight_copies(j):
            copy.start()
        return carry

    barrier = pltpu.get_barrier_semaphore()
    for other in (sib, xn, yn, dg):
        pl.semaphore_signal(barrier, inc=1, device_id=(other, c), device_id_type=MESH)

    @pl.when(c > 0)
    def _():
        pl.semaphore_signal(barrier, inc=1, device_id=(r, c - 1), device_id_type=MESH)

    @pl.when(c < 3)
    def _():
        pl.semaphore_signal(barrier, inc=1, device_id=(r, c + 1), device_id_type=MESH)

    lax.fori_loop(0, chunks, start_weights, 0)
    mine = pl.ds(pl.multiple_of(r * rows, rows), rows)
    locals_ = (
        pltpu.make_async_copy(act_ref, both.at[0, mine], own_sem.at[0]),
        pltpu.make_async_copy(grad_ref, both.at[1, mine], own_sem.at[1]),
    )
    for copy in locals_:
        copy.start()
    acc[...] = jnp.zeros_like(acc)

    end = (c == 0) | (c == 3)

    @pl.when(end)
    def _():
        pl.semaphore_wait(barrier, 5)

    @pl.when(jnp.logical_not(end))
    def _():
        pl.semaphore_wait(barrier, 6)

    def block(a, index):
        return both.at[a, pl.ds(pl.multiple_of(index * rows, rows), rows)]

    def gather(a, index, to, kind):
        return pltpu.make_async_remote_copy(
            src_ref=block(a, index), dst_ref=block(a, index),
            send_sem=gat_send.at[a, kind], recv_sem=gat_recv.at[a, kind],
            device_id=(to, c), device_id_type=MESH,
        )

    for copy in locals_:
        copy.wait()
    sent = []
    for a in (0, 1):
        sent += [gather(a, r, xn, 0), gather(a, r, yn, 1), gather(a, r, sib, 3)]
    for copy in sent:
        copy.start()
    gather(0, xn, xn, 0).wait_recv()
    sent.append(gather(0, xn, yn, 2))
    sent[-1].start()
    gather(1, yn, yn, 1).wait_recv()
    sent.append(gather(1, yn, xn, 2))
    sent[-1].start()
    for a, index, kind in ((0, xn, 4), (1, yn, 5)):
        sent.append(gather(a, index, sib, kind))
        sent[-1].start()
    gather(0, yn, yn, 1).wait_recv()
    gather(1, xn, xn, 0).wait_recv()
    for a, index, kind in ((0, yn, 5), (1, xn, 4)):
        sent.append(gather(a, index, sib, kind))
        sent[-1].start()
    for a in (0, 1):
        gather(a, dg, yn, 2).wait_recv()
        sent.append(gather(a, dg, sib, 6))
        sent[-1].start()
    for a in (0, 1):
        for kind, index in ((3, r), (4, xn), (5, yn), (6, dg)):
            gather(a, index + sib - r, sib, kind).wait_recv()

    act_out[...] = both[0]
    grad_out[...] = both[1]

    inner = jnp.where(c == 0, 1, 2)
    outer = jnp.where(c == 1, 0, 3)
    peer = 3 - c
    mine_h = jnp.where(c == 2, 1, 0)
    other_h = 1 - mine_h
    first_h = jnp.where(c == 0, 1, 0)

    def to_inner(j, h):
        return pltpu.make_async_remote_copy(
            src_ref=ep.at[j, h], dst_ref=rp.at[j, h], send_sem=ep_send.at[j, h], recv_sem=rp_recv.at[j, h],
            device_id=(r, inner), device_id_type=MESH,
        )

    def from_outer(j, h):
        return pltpu.make_async_remote_copy(
            src_ref=ep.at[j, h], dst_ref=rp.at[j, h], send_sem=ep_send.at[j, h], recv_sem=rp_recv.at[j, h],
            device_id=(r, outer), device_id_type=MESH,
        )

    def to_peer(j):
        return pltpu.make_async_remote_copy(
            src_ref=ep.at[j, other_h], dst_ref=xp.at[j], send_sem=xp_send.at[j], recv_sem=xp_recv.at[j],
            device_id=(r, peer), device_id_type=MESH,
        )

    def result(j, h, to, kind):
        return pltpu.make_async_remote_copy(
            src_ref=res.at[j, h], dst_ref=res.at[j, h], send_sem=res_send.at[kind, j], recv_sem=res_recv.at[j, h],
            device_id=(r, to), device_id_type=MESH,
        )

    def part(j):
        for copy in weight_copies(j):
            copy.wait()
        front = jnp.dot(both[0], wgu[j], preferred_element_type=jnp.float32)
        back = nt_dot(both[1], wdn[j])
        return jnp.concatenate([front, back], axis=1)

    def finish(j):
        cols = pl.ds(pl.multiple_of(j * CHUNK, CHUNK), CHUNK)
        ready = res[j].reshape(2 * half, 3 * CHUNK)
        hidden_out[:, cols] = ready[:, :CHUNK]
        gate_out[:, cols] = ready[:, CHUNK : 2 * CHUNK]
        up_out[:, cols] = ready[:, 2 * CHUNK :]
        for n in range(4):
            span = slice(n * width // 4, (n + 1) * width // 4)
            acc[:, span] += nt_dot(ready[:, CHUNK:], wgu[j, span, :])

    @pl.when(end)
    def _():
        def send(j, carry):
            total = part(j)
            ep[j] = total.astype(jnp.bfloat16).reshape(2, half, 3 * CHUNK)
            to_inner(j, first_h).start()
            to_inner(j, 1 - first_h).start()
            return carry

        def take(j, carry):
            for h in (0, 1):
                result(j, h, inner, 0).wait_recv()
            finish(j)
            return carry

        def drain(j, carry):
            for h in (0, 1):
                to_inner(j, h).wait_send()
            return carry

        lax.fori_loop(0, chunks, send, 0)
        lax.fori_loop(0, chunks, take, 0)
        lax.fori_loop(0, chunks, drain, 0)

    @pl.when(jnp.logical_not(end))
    def _():
        def step(i, carry):
            @pl.when(i <= last)
            def _():
                own[lax.rem(i, 2)] = part(i).reshape(2, half, 3 * CHUNK)
                from_outer(i, other_h).wait_recv()
                ep[i, other_h] = (
                    own[lax.rem(i, 2), other_h] + rp[i, other_h].astype(jnp.float32)
                ).astype(jnp.bfloat16)
                to_peer(i).start()

            @pl.when((i >= 1) & (i <= chunks))
            def _():
                j = i - 1
                from_outer(j, mine_h).wait_recv()
                to_peer(j).wait_recv()
                total = own[lax.rem(j, 2), mine_h] + (
                    rp[j, mine_h].astype(jnp.float32) + xp[j].astype(jnp.float32)
                )
                res[j, mine_h] = jnp.concatenate(swiglu_parts(total, CHUNK), axis=1)
                result(j, mine_h, peer, 0).start()
                result(j, mine_h, outer, 1).start()

            @pl.when(i >= 2)
            def _():
                j = i - 2
                result(j, other_h, peer, 0).wait_recv()
                result(j, other_h, outer, 2).start()
                finish(j)

            return carry

        def drain(j, carry):
            to_peer(j).wait_send()
            result(j, mine_h, peer, 0).wait_send()
            result(j, mine_h, outer, 1).wait_send()
            result(j, other_h, outer, 2).wait_send()
            return carry

        lax.fori_loop(0, chunks + 2, step, 0)
        lax.fori_loop(0, chunks, drain, 0)

    for copy in sent:
        copy.wait_send()

    def term(index):
        return pl.ds(pl.multiple_of(index * rows, rows), rows)

    def to_sib(k):
        return pltpu.make_async_remote_copy(
            src_ref=acc.at[term(2 * k + 1 - core)], dst_ref=pair.at[k],
            send_sem=pair_send.at[k], recv_sem=pair_recv.at[k],
            device_id=(sib, c), device_id_type=MESH,
        )

    for k in range(4):
        to_sib(k).start()
    for k in range(4):
        to_sib(k).wait_recv()

    def summed(index):
        return acc[term(index)] + pair[index // 2]

    def to_chip(kind, to):
        return pltpu.make_async_remote_copy(
            src_ref=send_buf.at[kind], dst_ref=recv_buf.at[kind],
            send_sem=rs_send.at[kind], recv_sem=rs_recv.at[kind],
            device_id=(to, c), device_id_type=MESH,
        )

    chips = ((2, dg), (0, xn), (1, yn))
    for kind, to in chips:
        send_buf[kind] = summed(to).astype(jnp.bfloat16)
        to_chip(kind, to).start()
    total = summed(r)
    for kind, to in chips:
        to_chip(kind, to).wait_recv()
        total += recv_buf[kind].astype(jnp.float32)
    in_grad_ref[...] = total.astype(jnp.bfloat16)
    for k in range(4):
        to_sib(k).wait_send()
    for kind, to in chips:
        to_chip(kind, to).wait_send()


def exchange(activations, out_grad, w_gate, w_up, w_down):
    rows, width = activations.shape
    hidden = w_gate.shape[1]
    tokens, chunks, half = 8 * rows, hidden // CHUNK, 4 * rows
    vmem = pl.BlockSpec(memory_space=pltpu.VMEM)
    anywhere = pl.BlockSpec(memory_space=pl.ANY)
    bf16, f32, dma = jnp.bfloat16, jnp.float32, pltpu.SemaphoreType.DMA
    return pl.pallas_call(
        exchange_kernel,
        out_shape=(
            jax.ShapeDtypeStruct((rows, width), bf16),
            jax.ShapeDtypeStruct((tokens, width), bf16),
            jax.ShapeDtypeStruct((tokens, width), bf16),
            jax.ShapeDtypeStruct((tokens, hidden), bf16),
            jax.ShapeDtypeStruct((tokens, hidden), bf16),
            jax.ShapeDtypeStruct((tokens, hidden), bf16),
        ),
        in_specs=[vmem, vmem, anywhere, anywhere, anywhere],
        out_specs=(vmem,) * 6,
        scratch_shapes=[
            pltpu.VMEM((2, tokens, width), bf16),
            pltpu.VMEM((chunks, width, 2 * CHUNK), bf16),
            pltpu.VMEM((chunks, CHUNK, width), bf16),
            pltpu.VMEM((chunks, 2, half, 3 * CHUNK), bf16),
            pltpu.VMEM((chunks, 2, half, 3 * CHUNK), bf16),
            pltpu.VMEM((chunks, half, 3 * CHUNK), bf16),
            pltpu.VMEM((chunks, 2, half, 3 * CHUNK), bf16),
            pltpu.VMEM((2, 2, half, 3 * CHUNK), f32),
            pltpu.VMEM((tokens, width), f32),
            pltpu.VMEM((4, rows, width), f32),
            pltpu.VMEM((3, rows, width), bf16),
            pltpu.VMEM((3, rows, width), bf16),
            dma((3, chunks)), dma((2, 7)), dma((2, 7)),
            dma((chunks, 2)), dma((chunks, 2)), dma((chunks,)), dma((chunks,)),
            dma((3, chunks)), dma((chunks, 2)),
            dma((4,)), dma((4,)), dma((3,)), dma((3,)), dma((2,)),
        ],
        compiler_params=pltpu.CompilerParams(
            collective_id=0, has_side_effects=True, vmem_limit_bytes=56 * 1024 * 1024
        ),
        cost_estimate=pl.CostEstimate(
            flops=10 * tokens * width * hidden,
            bytes_accessed=6 * width * hidden,
            transcendentals=tokens * hidden,
        ),
    )(activations, out_grad, w_gate, w_up, w_down)


def outer_kernel(split, act_ref, grad_ref, hidden_ref, gate_ref, up_ref, gate_out, up_out, down_out):
    i = pl.program_id(0)

    @pl.when(i < split)
    def _():
        gate_out[...] = tn_dot(act_ref[...], gate_ref[...]).astype(jnp.bfloat16)
        up_out[...] = tn_dot(act_ref[...], up_ref[...]).astype(jnp.bfloat16)

    @pl.when(i >= split)
    def _():
        down_out[...] = tn_dot(hidden_ref[...], grad_ref[...]).astype(jnp.bfloat16)


def outer_products(act, grad, hidden, gate_grad, up_grad):
    tokens, width = act.shape
    units = hidden.shape[1]
    tile = 256
    split = width // tile
    early = lambda i: jnp.minimum(i, split - 1)
    late = lambda i: jnp.maximum(i - split, 0)
    whole = lambda i: (0, 0)
    return pl.pallas_call(
        functools.partial(outer_kernel, split),
        grid=(split + units // tile,),
        out_shape=(
            jax.ShapeDtypeStruct((width, units), jnp.bfloat16),
            jax.ShapeDtypeStruct((width, units), jnp.bfloat16),
            jax.ShapeDtypeStruct((units, width), jnp.bfloat16),
        ),
        in_specs=[
            pl.BlockSpec((tokens, tile), lambda i: (0, early(i))),
            pl.BlockSpec((tokens, width), whole),
            pl.BlockSpec((tokens, tile), lambda i: (0, late(i))),
            pl.BlockSpec((tokens, units), whole),
            pl.BlockSpec((tokens, units), whole),
        ],
        out_specs=(
            pl.BlockSpec((tile, units), lambda i: (early(i), 0)),
            pl.BlockSpec((tile, units), lambda i: (early(i), 0)),
            pl.BlockSpec((tile, width), lambda i: (late(i), 0)),
        ),
        compiler_params=pltpu.CompilerParams(vmem_limit_bytes=40 * 1024 * 1024),
        cost_estimate=pl.CostEstimate(
            flops=6 * tokens * width * units,
            bytes_accessed=6 * width * units,
            transcendentals=0,
        ),
    )(act, grad, hidden, gate_grad, up_grad)


def on_device_fused(activations, out_grad, w_gate, w_up, w_down):
    in_grad, act, grad, hidden, gate_grad, up_grad = exchange(
        activations, out_grad, w_gate, w_up, w_down
    )
    grad_gate, grad_up, grad_down = outer_products(act, grad, hidden, gate_grad, up_grad)
    return (in_grad, grad_gate, grad_up, grad_down)


def solution(mesh):
    placed = (P("row", "col"), P("row", "col"), P("col", "row"), P("col", "row"), P("row", "col"))
    fused = mesh.axis_names == ("row", "col") and dict(mesh.shape) == {"row": 8, "col": 4}
    return jax.shard_map(
        on_device_fused if fused else on_device,
        mesh=mesh,
        in_specs=placed,
        out_specs=(P("row", "col"), P("col", "row"), P("col", "row"), P("row", "col")),
        check_vma=False,
    )
```

```python
import functools

import jax
import jax.numpy as jnp
from jax import lax
from jax.experimental import pallas as pl
from jax.experimental.pallas import tpu as pltpu
from jax.sharding import PartitionSpec as P


def swiglu_parts(summed, width):
    gate = summed[:, :width]
    up_val = summed[:, width : 2 * width]
    hidden_grad = summed[:, 2 * width :]
    sigma = jax.nn.sigmoid(gate)
    hidden = (gate * sigma * up_val).astype(jnp.bfloat16)
    up_grad = (hidden_grad * gate * sigma).astype(jnp.bfloat16)
    gate_grad = (hidden_grad * up_val * sigma * (1.0 + gate * (1.0 - sigma))).astype(jnp.bfloat16)
    return (hidden, gate_grad, up_grad)


def on_device(activations, out_grad, w_gate, w_up, w_down):
    inputs, grads = (
        lax.all_gather(activations, "row", axis=0, tiled=True),
        lax.all_gather(out_grad, "row", axis=0, tiled=True),
    )
    width = w_gate.shape[1]
    contract_last = (((1,), (1,)), ((), ()))
    contract_first = (((0,), (0,)), ((), ()))
    gate_part = jnp.dot(inputs, w_gate, preferred_element_type=jnp.float32)
    up_part = jnp.dot(inputs, w_up, preferred_element_type=jnp.float32)
    back_part = lax.dot_general(grads, w_down, contract_last, preferred_element_type=jnp.float32)
    summed = lax.psum(jnp.concatenate([gate_part, up_part, back_part], axis=1), "col")
    hidden, gate_grad, up_grad = swiglu_parts(summed, width)
    grad_down = lax.dot_general(
        hidden, grads, contract_first, preferred_element_type=jnp.float32
    ).astype(jnp.bfloat16)
    grad_gate = lax.dot_general(
        inputs, gate_grad, contract_first, preferred_element_type=jnp.float32
    ).astype(jnp.bfloat16)
    grad_up = lax.dot_general(
        inputs, up_grad, contract_first, preferred_element_type=jnp.float32
    ).astype(jnp.bfloat16)
    term = lax.dot_general(gate_grad, w_gate, contract_last, preferred_element_type=jnp.float32)
    in_grad = lax.psum_scatter(
        term + lax.dot_general(up_grad, w_up, contract_last, preferred_element_type=jnp.float32),
        "row",
        scatter_dimension=0,
        tiled=True,
    ).astype(jnp.bfloat16)
    return (in_grad, grad_gate, grad_up, grad_down)


MESH = pl.DeviceIdType.MESH
CHUNK = 128


def exchange_kernel(
    act_ref, grad_ref, wg_ref, wu_ref, wd_ref,
    in_grad_ref, act_t_out, grad_out, hidden_t_out, gate_out, up_out,
    both, grad_t, wgu, wdn, ep, rp, xp, res, own, acc_t, acc, pair, send_buf, recv_buf,
    w_sem, gat_send, gat_recv, ep_send, rp_recv, xp_send, xp_recv, res_send, res_recv,
    pair_send, pair_recv, rs_send, rs_recv, own_sem,
):
    chunks = wgu.shape[0]
    rows, width = act_ref.shape
    half = rows * 4
    r = lax.axis_index("row")
    c = lax.axis_index("col")
    core = lax.rem(r, 2)
    x = lax.rem(r // 2, 2)
    y = r // 4
    sib = r + 1 - 2 * core
    xn = r + 2 - 4 * x
    yn = r + 4 - 8 * y
    dg = xn + 4 - 8 * y
    last = chunks - 1

    def weight_copies(j):
        cols = pl.ds(pl.multiple_of(j * CHUNK, CHUNK), CHUNK)
        return (
            pltpu.make_async_copy(wg_ref.at[:, cols], wgu.at[j, :, pl.ds(0, CHUNK)], w_sem.at[0, j]),
            pltpu.make_async_copy(wu_ref.at[:, cols], wgu.at[j, :, pl.ds(CHUNK, CHUNK)], w_sem.at[1, j]),
            pltpu.make_async_copy(wd_ref.at[cols, :], wdn.at[j], w_sem.at[2, j]),
        )

    def start_weights(j, carry):
        for copy in weight_copies(j):
            copy.start()
        return carry

    barrier = pltpu.get_barrier_semaphore()
    for other in (sib, xn, yn, dg):
        pl.semaphore_signal(barrier, inc=1, device_id=(other, c), device_id_type=MESH)

    @pl.when(c > 0)
    def _():
        pl.semaphore_signal(barrier, inc=1, device_id=(r, c - 1), device_id_type=MESH)

    @pl.when(c < 3)
    def _():
        pl.semaphore_signal(barrier, inc=1, device_id=(r, c + 1), device_id_type=MESH)

    lax.fori_loop(0, chunks, start_weights, 0)
    mine = pl.ds(pl.multiple_of(r * rows, rows), rows)
    locals_ = (
        pltpu.make_async_copy(act_ref, both.at[0, mine], own_sem.at[0]),
        pltpu.make_async_copy(grad_ref, both.at[1, mine], own_sem.at[1]),
    )
    for copy in locals_:
        copy.start()
    acc_t[...] = jnp.zeros_like(acc_t)

    end = (c == 0) | (c == 3)

    @pl.when(end)
    def _():
        pl.semaphore_wait(barrier, 5)

    @pl.when(jnp.logical_not(end))
    def _():
        pl.semaphore_wait(barrier, 6)

    def block(a, index):
        return both.at[a, pl.ds(pl.multiple_of(index * rows, rows), rows)]

    def gather(a, index, to, kind):
        return pltpu.make_async_remote_copy(
            src_ref=block(a, index), dst_ref=block(a, index),
            send_sem=gat_send.at[a, kind], recv_sem=gat_recv.at[a, kind],
            device_id=(to, c), device_id_type=MESH,
        )

    for copy in locals_:
        copy.wait()
    sent = []
    for a in (0, 1):
        sent += [gather(a, r, xn, 0), gather(a, r, yn, 1), gather(a, r, sib, 3)]
    for copy in sent:
        copy.start()
    gather(0, xn, xn, 0).wait_recv()
    sent.append(gather(0, xn, yn, 2))
    sent[-1].start()
    gather(1, yn, yn, 1).wait_recv()
    sent.append(gather(1, yn, xn, 2))
    sent[-1].start()
    for a, index, kind in ((0, xn, 4), (1, yn, 5)):
        sent.append(gather(a, index, sib, kind))
        sent[-1].start()
    gather(0, yn, yn, 1).wait_recv()
    gather(1, xn, xn, 0).wait_recv()
    for a, index, kind in ((0, yn, 5), (1, xn, 4)):
        sent.append(gather(a, index, sib, kind))
        sent[-1].start()
    for a in (0, 1):
        gather(a, dg, yn, 2).wait_recv()
        sent.append(gather(a, dg, sib, 6))
        sent[-1].start()
    for a in (0, 1):
        for kind, index in ((3, r), (4, xn), (5, yn), (6, dg)):
            gather(a, index + sib - r, sib, kind).wait_recv()

    grad_t[...] = both[1].T

    inner = jnp.where(c == 0, 1, 2)
    outer = jnp.where(c == 1, 0, 3)
    peer = 3 - c
    mine_h = jnp.where(c == 2, 1, 0)
    other_h = 1 - mine_h
    first_h = jnp.where(c == 0, 1, 0)

    def to_inner(j, h):
        return pltpu.make_async_remote_copy(
            src_ref=ep.at[j, h], dst_ref=rp.at[j, h], send_sem=ep_send.at[j, h], recv_sem=rp_recv.at[j, h],
            device_id=(r, inner), device_id_type=MESH,
        )

    def from_outer(j, h):
        return pltpu.make_async_remote_copy(
            src_ref=ep.at[j, h], dst_ref=rp.at[j, h], send_sem=ep_send.at[j, h], recv_sem=rp_recv.at[j, h],
            device_id=(r, outer), device_id_type=MESH,
        )

    def to_peer(j):
        return pltpu.make_async_remote_copy(
            src_ref=ep.at[j, other_h], dst_ref=xp.at[j], send_sem=xp_send.at[j], recv_sem=xp_recv.at[j],
            device_id=(r, peer), device_id_type=MESH,
        )

    def result(j, h, to, kind):
        return pltpu.make_async_remote_copy(
            src_ref=res.at[j, h], dst_ref=res.at[j, h], send_sem=res_send.at[kind, j], recv_sem=res_recv.at[j, h],
            device_id=(r, to), device_id_type=MESH,
        )

    def part(j):
        for copy in weight_copies(j):
            copy.wait()
        front = jnp.dot(both[0], wgu[j], preferred_element_type=jnp.float32)
        back = jnp.dot(wdn[j], grad_t[...], preferred_element_type=jnp.float32)
        return jnp.concatenate([front, back.T], axis=1)

    def finish(j):
        cols = pl.ds(pl.multiple_of(j * CHUNK, CHUNK), CHUNK)
        ready = res[j].reshape(2 * half, 3 * CHUNK)
        hidden_t_out[cols, :] = ready[:, :CHUNK].T
        gate_out[:, cols] = ready[:, CHUNK : 2 * CHUNK]
        up_out[:, cols] = ready[:, 2 * CHUNK :]
        both_t = ready[:, CHUNK:].T
        for n in range(4):
            span = slice(n * width // 4, (n + 1) * width // 4)
            acc_t[span, :] += jnp.dot(wgu[j, span, :], both_t, preferred_element_type=jnp.float32)

        @pl.when(j < 8)
        def _():
            span = pl.ds(pl.multiple_of(j * (width // 8), width // 8), width // 8)
            act_t_out[span, :] = both[0, :, span].T
            grad_out[:, span] = both[1, :, span]

    @pl.when(end)
    def _():
        def send(j, carry):
            total = part(j)
            ep[j] = total.astype(jnp.bfloat16).reshape(2, half, 3 * CHUNK)
            to_inner(j, first_h).start()
            to_inner(j, 1 - first_h).start()
            return carry

        def take(j, carry):
            for h in (0, 1):
                result(j, h, inner, 0).wait_recv()
            finish(j)
            return carry

        def drain(j, carry):
            for h in (0, 1):
                to_inner(j, h).wait_send()
            return carry

        lax.fori_loop(0, chunks, send, 0)
        lax.fori_loop(0, chunks, take, 0)
        lax.fori_loop(0, chunks, drain, 0)

    @pl.when(jnp.logical_not(end))
    def _():
        def step(i, carry):
            @pl.when(i <= last)
            def _():
                own[lax.rem(i, 2)] = part(i).reshape(2, half, 3 * CHUNK)
                from_outer(i, other_h).wait_recv()
                ep[i, other_h] = (
                    own[lax.rem(i, 2), other_h] + rp[i, other_h].astype(jnp.float32)
                ).astype(jnp.bfloat16)
                to_peer(i).start()

            @pl.when((i >= 1) & (i <= chunks))
            def _():
                j = i - 1
                from_outer(j, mine_h).wait_recv()
                to_peer(j).wait_recv()
                total = own[lax.rem(j, 2), mine_h] + (
                    rp[j, mine_h].astype(jnp.float32) + xp[j].astype(jnp.float32)
                )
                res[j, mine_h] = jnp.concatenate(swiglu_parts(total, CHUNK), axis=1)
                result(j, mine_h, peer, 0).start()
                result(j, mine_h, outer, 1).start()

            @pl.when(i >= 2)
            def _():
                j = i - 2
                result(j, other_h, peer, 0).wait_recv()
                result(j, other_h, outer, 2).start()
                finish(j)

            return carry

        def drain(j, carry):
            to_peer(j).wait_send()
            result(j, mine_h, peer, 0).wait_send()
            result(j, mine_h, outer, 1).wait_send()
            result(j, other_h, outer, 2).wait_send()
            return carry

        lax.fori_loop(0, chunks + 2, step, 0)
        lax.fori_loop(0, chunks, drain, 0)

    for copy in sent:
        copy.wait_send()

    acc[...] = acc_t[...].T

    def term(index):
        return pl.ds(pl.multiple_of(index * rows, rows), rows)

    def to_sib(k):
        return pltpu.make_async_remote_copy(
            src_ref=acc.at[term(2 * k + 1 - core)], dst_ref=pair.at[k],
            send_sem=pair_send.at[k], recv_sem=pair_recv.at[k],
            device_id=(sib, c), device_id_type=MESH,
        )

    for k in range(4):
        to_sib(k).start()
    for k in range(4):
        to_sib(k).wait_recv()

    def summed(index):
        return acc[term(index)] + pair[index // 2]

    def to_chip(kind, to):
        return pltpu.make_async_remote_copy(
            src_ref=send_buf.at[kind], dst_ref=recv_buf.at[kind],
            send_sem=rs_send.at[kind], recv_sem=rs_recv.at[kind],
            device_id=(to, c), device_id_type=MESH,
        )

    chips = ((2, dg), (0, xn), (1, yn))
    for kind, to in chips:
        send_buf[kind] = summed(to).astype(jnp.bfloat16)
        to_chip(kind, to).start()
    total = summed(r)
    for kind, to in chips:
        to_chip(kind, to).wait_recv()
        total += recv_buf[kind].astype(jnp.float32)
    in_grad_ref[...] = total.astype(jnp.bfloat16)
    for k in range(4):
        to_sib(k).wait_send()
    for kind, to in chips:
        to_chip(kind, to).wait_send()


def exchange(activations, out_grad, w_gate, w_up, w_down):
    rows, width = activations.shape
    hidden = w_gate.shape[1]
    tokens, chunks, half = 8 * rows, hidden // CHUNK, 4 * rows
    vmem = pl.BlockSpec(memory_space=pltpu.VMEM)
    anywhere = pl.BlockSpec(memory_space=pl.ANY)
    bf16, f32, dma = jnp.bfloat16, jnp.float32, pltpu.SemaphoreType.DMA
    return pl.pallas_call(
        exchange_kernel,
        out_shape=(
            jax.ShapeDtypeStruct((rows, width), bf16),
            jax.ShapeDtypeStruct((width, tokens), bf16),
            jax.ShapeDtypeStruct((tokens, width), bf16),
            jax.ShapeDtypeStruct((hidden, tokens), bf16),
            jax.ShapeDtypeStruct((tokens, hidden), bf16),
            jax.ShapeDtypeStruct((tokens, hidden), bf16),
        ),
        in_specs=[vmem, vmem, anywhere, anywhere, anywhere],
        out_specs=(vmem,) * 6,
        scratch_shapes=[
            pltpu.VMEM((2, tokens, width), bf16),
            pltpu.VMEM((width, tokens), bf16),
            pltpu.VMEM((chunks, width, 2 * CHUNK), bf16),
            pltpu.VMEM((chunks, CHUNK, width), bf16),
            pltpu.VMEM((chunks, 2, half, 3 * CHUNK), bf16),
            pltpu.VMEM((chunks, 2, half, 3 * CHUNK), bf16),
            pltpu.VMEM((chunks, half, 3 * CHUNK), bf16),
            pltpu.VMEM((chunks, 2, half, 3 * CHUNK), bf16),
            pltpu.VMEM((2, 2, half, 3 * CHUNK), f32),
            pltpu.VMEM((width, tokens), f32),
            pltpu.VMEM((tokens, width), f32),
            pltpu.VMEM((4, rows, width), f32),
            pltpu.VMEM((3, rows, width), bf16),
            pltpu.VMEM((3, rows, width), bf16),
            dma((3, chunks)), dma((2, 7)), dma((2, 7)),
            dma((chunks, 2)), dma((chunks, 2)), dma((chunks,)), dma((chunks,)),
            dma((3, chunks)), dma((chunks, 2)),
            dma((4,)), dma((4,)), dma((3,)), dma((3,)), dma((2,)),
        ],
        compiler_params=pltpu.CompilerParams(
            collective_id=0, has_side_effects=True, vmem_limit_bytes=56 * 1024 * 1024
        ),
        cost_estimate=pl.CostEstimate(
            flops=10 * tokens * width * hidden,
            bytes_accessed=6 * width * hidden,
            transcendentals=tokens * hidden,
        ),
    )(activations, out_grad, w_gate, w_up, w_down)


def outer_kernel(act_t_ref, grad_ref, hidden_t_ref, gate_ref, up_ref, gate_out, up_out, down_out):
    tile = 256
    for left, right, out in (
        (act_t_ref, gate_ref, gate_out),
        (act_t_ref, up_ref, up_out),
        (hidden_t_ref, grad_ref, down_out),
    ):
        for n in range(out.shape[1] // tile):
            span = slice(n * tile, (n + 1) * tile)
            out[:, span] = jnp.dot(
                left[...], right[:, span], preferred_element_type=jnp.float32
            ).astype(jnp.bfloat16)


def outer_products(act_t, grad, hidden_t, gate_grad, up_grad):
    width, tokens = act_t.shape
    units = hidden_t.shape[0]
    steps = 8
    down = lambda i: (i, 0)
    whole = lambda i: (0, 0)
    return pl.pallas_call(
        outer_kernel,
        grid=(steps,),
        out_shape=(
            jax.ShapeDtypeStruct((width, units), jnp.bfloat16),
            jax.ShapeDtypeStruct((width, units), jnp.bfloat16),
            jax.ShapeDtypeStruct((units, width), jnp.bfloat16),
        ),
        in_specs=[
            pl.BlockSpec((width // steps, tokens), down),
            pl.BlockSpec((tokens, width), whole),
            pl.BlockSpec((units // steps, tokens), down),
            pl.BlockSpec((tokens, units), whole),
            pl.BlockSpec((tokens, units), whole),
        ],
        out_specs=(
            pl.BlockSpec((width // steps, units), down),
            pl.BlockSpec((width // steps, units), down),
            pl.BlockSpec((units // steps, width), down),
        ),
        compiler_params=pltpu.CompilerParams(vmem_limit_bytes=60 * 1024 * 1024),
        cost_estimate=pl.CostEstimate(
            flops=6 * tokens * width * units,
            bytes_accessed=6 * width * units,
            transcendentals=0,
        ),
    )(act_t, grad, hidden_t, gate_grad, up_grad)


def on_device_fused(activations, out_grad, w_gate, w_up, w_down):
    in_grad, act_t, grad, hidden_t, gate_grad, up_grad = exchange(
        activations, out_grad, w_gate, w_up, w_down
    )
    grad_gate, grad_up, grad_down = outer_products(act_t, grad, hidden_t, gate_grad, up_grad)
    return (in_grad, grad_gate, grad_up, grad_down)


def solution(mesh):
    placed = (P("row", "col"), P("row", "col"), P("col", "row"), P("col", "row"), P("row", "col"))
    fused = mesh.axis_names == ("row", "col") and dict(mesh.shape) == {"row": 8, "col": 4}
    return jax.shard_map(
        on_device_fused if fused else on_device,
        mesh=mesh,
        in_specs=placed,
        out_specs=(P("row", "col"), P("col", "row"), P("col", "row"), P("row", "col")),
        check_vma=False,
    )
```

```python
import functools

import jax
import jax.numpy as jnp
from jax import lax
from jax.experimental import pallas as pl
from jax.experimental.pallas import tpu as pltpu
from jax.sharding import PartitionSpec as P


def swiglu_parts(summed, width):
    gate = summed[:, :width]
    up_val = summed[:, width : 2 * width]
    hidden_grad = summed[:, 2 * width :]
    sigma = jax.nn.sigmoid(gate)
    hidden = (gate * sigma * up_val).astype(jnp.bfloat16)
    up_grad = (hidden_grad * gate * sigma).astype(jnp.bfloat16)
    gate_grad = (hidden_grad * up_val * sigma * (1.0 + gate * (1.0 - sigma))).astype(jnp.bfloat16)
    return (hidden, gate_grad, up_grad)


def on_device(activations, out_grad, w_gate, w_up, w_down):
    inputs, grads = (
        lax.all_gather(activations, "row", axis=0, tiled=True),
        lax.all_gather(out_grad, "row", axis=0, tiled=True),
    )
    width = w_gate.shape[1]
    contract_last = (((1,), (1,)), ((), ()))
    contract_first = (((0,), (0,)), ((), ()))
    gate_part = jnp.dot(inputs, w_gate, preferred_element_type=jnp.float32)
    up_part = jnp.dot(inputs, w_up, preferred_element_type=jnp.float32)
    back_part = lax.dot_general(grads, w_down, contract_last, preferred_element_type=jnp.float32)
    summed = lax.psum(jnp.concatenate([gate_part, up_part, back_part], axis=1), "col")
    hidden, gate_grad, up_grad = swiglu_parts(summed, width)
    grad_down = lax.dot_general(
        hidden, grads, contract_first, preferred_element_type=jnp.float32
    ).astype(jnp.bfloat16)
    grad_gate = lax.dot_general(
        inputs, gate_grad, contract_first, preferred_element_type=jnp.float32
    ).astype(jnp.bfloat16)
    grad_up = lax.dot_general(
        inputs, up_grad, contract_first, preferred_element_type=jnp.float32
    ).astype(jnp.bfloat16)
    term = lax.dot_general(gate_grad, w_gate, contract_last, preferred_element_type=jnp.float32)
    in_grad = lax.psum_scatter(
        term + lax.dot_general(up_grad, w_up, contract_last, preferred_element_type=jnp.float32),
        "row",
        scatter_dimension=0,
        tiled=True,
    ).astype(jnp.bfloat16)
    return (in_grad, grad_gate, grad_up, grad_down)


MESH = pl.DeviceIdType.MESH
CHUNK = 128
ADD_LAG, PASS_LAG = 2, 4


def nt_dot(a, b):
    return lax.dot_general(a, b, (((1,), (1,)), ((), ())), preferred_element_type=jnp.float32)


def tn_dot(a, b):
    return lax.dot_general(a, b, (((0,), (0,)), ((), ())), preferred_element_type=jnp.float32)


def exchange_kernel(
    act_ref, grad_ref, wg_ref, wu_ref, wd_ref,
    mine_ref, x_ref, y_ref, diag_ref, act_t_out, grad_out, hidden_t_out, gate_out, up_out,
    both, wgu, wdn, ep, rp, xp, res, own, acc, pair,
    w_sem, gat_send, gat_recv, ep_send, rp_recv, xp_send, xp_recv, res_send, res_recv,
    pair_send, pair_recv, own_sem,
):
    chip_refs = (x_ref, y_ref, diag_ref)
    chunks = wgu.shape[0]
    rows, width = act_ref.shape
    half = rows * 4
    r = lax.axis_index("row")
    c = lax.axis_index("col")
    core = lax.rem(r, 2)
    x = lax.rem(r // 2, 2)
    y = r // 4
    sib = r + 1 - 2 * core
    xn = r + 2 - 4 * x
    yn = r + 4 - 8 * y
    dg = xn + 4 - 8 * y
    last = chunks - 1

    def weight_copies(j):
        cols = pl.ds(pl.multiple_of(j * CHUNK, CHUNK), CHUNK)
        return (
            pltpu.make_async_copy(wg_ref.at[:, cols], wgu.at[j, :, pl.ds(0, CHUNK)], w_sem.at[0, j]),
            pltpu.make_async_copy(wu_ref.at[:, cols], wgu.at[j, :, pl.ds(CHUNK, CHUNK)], w_sem.at[1, j]),
            pltpu.make_async_copy(wd_ref.at[cols, :], wdn.at[j], w_sem.at[2, j]),
        )

    def start_weights(j, carry):
        for copy in weight_copies(j):
            copy.start()
        return carry

    barrier = pltpu.get_barrier_semaphore()
    for other in (sib, xn, yn, dg):
        pl.semaphore_signal(barrier, inc=1, device_id=(other, c), device_id_type=MESH)

    @pl.when(c > 0)
    def _():
        pl.semaphore_signal(barrier, inc=1, device_id=(r, c - 1), device_id_type=MESH)

    @pl.when(c < 3)
    def _():
        pl.semaphore_signal(barrier, inc=1, device_id=(r, c + 1), device_id_type=MESH)

    lax.fori_loop(0, chunks, start_weights, 0)
    mine = pl.ds(pl.multiple_of(r * rows, rows), rows)
    locals_ = (
        pltpu.make_async_copy(act_ref, both.at[0, mine], own_sem.at[0]),
        pltpu.make_async_copy(grad_ref, both.at[1, mine], own_sem.at[1]),
    )
    for copy in locals_:
        copy.start()
    acc[...] = jnp.zeros_like(acc)

    end = (c == 0) | (c == 3)

    @pl.when(end)
    def _():
        pl.semaphore_wait(barrier, 5)

    @pl.when(jnp.logical_not(end))
    def _():
        pl.semaphore_wait(barrier, 6)

    def block(a, index):
        return both.at[a, pl.ds(pl.multiple_of(index * rows, rows), rows)]

    def gather(a, index, to, kind):
        return pltpu.make_async_remote_copy(
            src_ref=block(a, index), dst_ref=block(a, index),
            send_sem=gat_send.at[a, kind], recv_sem=gat_recv.at[a, kind],
            device_id=(to, c), device_id_type=MESH,
        )

    for copy in locals_:
        copy.wait()
    sent = []
    for a in (0, 1):
        sent += [gather(a, r, xn, 0), gather(a, r, yn, 1), gather(a, r, sib, 3)]
    for copy in sent:
        copy.start()
    gather(0, xn, xn, 0).wait_recv()
    sent.append(gather(0, xn, yn, 2))
    sent[-1].start()
    gather(1, yn, yn, 1).wait_recv()
    sent.append(gather(1, yn, xn, 2))
    sent[-1].start()
    for a, index, kind in ((0, xn, 4), (1, yn, 5)):
        sent.append(gather(a, index, sib, kind))
        sent[-1].start()
    gather(0, yn, yn, 1).wait_recv()
    gather(1, xn, xn, 0).wait_recv()
    for a, index, kind in ((0, yn, 5), (1, xn, 4)):
        sent.append(gather(a, index, sib, kind))
        sent[-1].start()
    for a in (0, 1):
        gather(a, dg, yn, 2).wait_recv()
        sent.append(gather(a, dg, sib, 6))
        sent[-1].start()
    for a in (0, 1):
        for kind, index in ((3, r), (4, xn), (5, yn), (6, dg)):
            gather(a, index + sib - r, sib, kind).wait_recv()

    inner = jnp.where(c == 0, 1, 2)
    outer = jnp.where(c == 1, 0, 3)
    peer = 3 - c
    mine_h = jnp.where(c == 2, 1, 0)
    other_h = 1 - mine_h
    first_h = jnp.where(c == 0, 1, 0)

    def to_inner(j, h):
        return pltpu.make_async_remote_copy(
            src_ref=ep.at[j, h], dst_ref=rp.at[j, h], send_sem=ep_send.at[j, h], recv_sem=rp_recv.at[j, h],
            device_id=(r, inner), device_id_type=MESH,
        )

    def from_outer(j, h):
        return pltpu.make_async_remote_copy(
            src_ref=ep.at[j, h], dst_ref=rp.at[j, h], send_sem=ep_send.at[j, h], recv_sem=rp_recv.at[j, h],
            device_id=(r, outer), device_id_type=MESH,
        )

    def to_peer(j):
        return pltpu.make_async_remote_copy(
            src_ref=ep.at[j, other_h], dst_ref=xp.at[j], send_sem=xp_send.at[j], recv_sem=xp_recv.at[j],
            device_id=(r, peer), device_id_type=MESH,
        )

    def result(j, h, to, kind):
        return pltpu.make_async_remote_copy(
            src_ref=res.at[j, h], dst_ref=res.at[j, h], send_sem=res_send.at[kind, j], recv_sem=res_recv.at[j, h],
            device_id=(r, to), device_id_type=MESH,
        )

    def part(j):
        for copy in weight_copies(j):
            copy.wait()
        front = jnp.dot(both[0], wgu[j], preferred_element_type=jnp.float32)
        back = nt_dot(both[1], wdn[j])
        return jnp.concatenate([front, back], axis=1)

    def finish(j):
        cols = pl.ds(pl.multiple_of(j * CHUNK, CHUNK), CHUNK)
        ready = res[j].reshape(2 * half, 3 * CHUNK)
        hidden_t_out[cols, :] = ready[:, :CHUNK].T
        gate_out[:, cols] = ready[:, CHUNK : 2 * CHUNK]
        up_out[:, cols] = ready[:, 2 * CHUNK :]
        for n in range(4):
            span = slice(n * width // 4, (n + 1) * width // 4)
            acc[:, span] += nt_dot(ready[:, CHUNK:], wgu[j, span, :])

        @pl.when(j < 8)
        def _():
            span = pl.ds(pl.multiple_of(j * (width // 8), width // 8), width // 8)
            act_t_out[span, :] = both[0, :, span].T
            grad_out[:, span] = both[1, :, span]

    @pl.when(end)
    def _():
        def send(j, carry):
            total = part(j)
            ep[j] = total.astype(jnp.bfloat16).reshape(2, half, 3 * CHUNK)
            to_inner(j, first_h).start()
            to_inner(j, 1 - first_h).start()
            return carry

        def take(j, carry):
            for h in (0, 1):
                result(j, h, inner, 0).wait_recv()
            finish(j)
            return carry

        def drain(j, carry):
            for h in (0, 1):
                to_inner(j, h).wait_send()
            return carry

        lax.fori_loop(0, chunks, send, 0)
        lax.fori_loop(0, chunks, take, 0)
        lax.fori_loop(0, chunks, drain, 0)

    @pl.when(jnp.logical_not(end))
    def _():
        def step(i, carry):
            @pl.when(i <= last)
            def _():
                own[lax.rem(i, 4)] = part(i).reshape(2, half, 3 * CHUNK)
                from_outer(i, other_h).wait_recv()
                ep[i, other_h] = (
                    own[lax.rem(i, 4), other_h] + rp[i, other_h].astype(jnp.float32)
                ).astype(jnp.bfloat16)
                to_peer(i).start()

            @pl.when((i >= ADD_LAG) & (i < chunks + ADD_LAG))
            def _():
                j = i - ADD_LAG
                from_outer(j, mine_h).wait_recv()
                to_peer(j).wait_recv()
                total = own[lax.rem(j, 4), mine_h] + (
                    rp[j, mine_h].astype(jnp.float32) + xp[j].astype(jnp.float32)
                )
                res[j, mine_h] = jnp.concatenate(swiglu_parts(total, CHUNK), axis=1)
                result(j, mine_h, peer, 0).start()
                result(j, mine_h, outer, 1).start()

            @pl.when(i >= PASS_LAG)
            def _():
                j = i - PASS_LAG
                result(j, other_h, peer, 0).wait_recv()
                result(j, other_h, outer, 2).start()
                finish(j)

            return carry

        def drain(j, carry):
            to_peer(j).wait_send()
            result(j, mine_h, peer, 0).wait_send()
            result(j, mine_h, outer, 1).wait_send()
            result(j, other_h, outer, 2).wait_send()
            return carry

        lax.fori_loop(0, chunks + PASS_LAG, step, 0)
        lax.fori_loop(0, chunks, drain, 0)

    for copy in sent:
        copy.wait_send()

    def term(index):
        return pl.ds(pl.multiple_of(index * rows, rows), rows)

    def to_sib(k):
        return pltpu.make_async_remote_copy(
            src_ref=acc.at[term(2 * k + 1 - core)], dst_ref=pair.at[k],
            send_sem=pair_send.at[k], recv_sem=pair_recv.at[k],
            device_id=(sib, c), device_id_type=MESH,
        )

    for k in range(4):
        to_sib(k).start()
    for k in range(4):
        to_sib(k).wait_recv()

    def summed(index):
        return acc[term(index)] + pair[index // 2]

    mine_ref[...] = summed(r)
    for kind, to in enumerate((xn, yn, dg)):
        chip_refs[kind][...] = summed(to).astype(jnp.bfloat16)
    for k in range(4):
        to_sib(k).wait_send()


def exchange(activations, out_grad, w_gate, w_up, w_down):
    rows, width = activations.shape
    hidden = w_gate.shape[1]
    tokens, chunks, half = 8 * rows, hidden // CHUNK, 4 * rows
    vmem = pl.BlockSpec(memory_space=pltpu.VMEM)
    anywhere = pl.BlockSpec(memory_space=pl.ANY)
    bf16, f32, dma = jnp.bfloat16, jnp.float32, pltpu.SemaphoreType.DMA
    return pl.pallas_call(
        exchange_kernel,
        out_shape=(
            jax.ShapeDtypeStruct((rows, width), f32),
            jax.ShapeDtypeStruct((rows, width), bf16),
            jax.ShapeDtypeStruct((rows, width), bf16),
            jax.ShapeDtypeStruct((rows, width), bf16),
            jax.ShapeDtypeStruct((width, tokens), bf16),
            jax.ShapeDtypeStruct((tokens, width), bf16),
            jax.ShapeDtypeStruct((hidden, tokens), bf16),
            jax.ShapeDtypeStruct((tokens, hidden), bf16),
            jax.ShapeDtypeStruct((tokens, hidden), bf16),
        ),
        in_specs=[vmem, vmem, anywhere, anywhere, anywhere],
        out_specs=(vmem,) * 9,
        scratch_shapes=[
            pltpu.VMEM((2, tokens, width), bf16),
            pltpu.VMEM((chunks, width, 2 * CHUNK), bf16),
            pltpu.VMEM((chunks, CHUNK, width), bf16),
            pltpu.VMEM((chunks, 2, half, 3 * CHUNK), bf16),
            pltpu.VMEM((chunks, 2, half, 3 * CHUNK), bf16),
            pltpu.VMEM((chunks, half, 3 * CHUNK), bf16),
            pltpu.VMEM((chunks, 2, half, 3 * CHUNK), bf16),
            pltpu.VMEM((4, 2, half, 3 * CHUNK), f32),
            pltpu.VMEM((tokens, width), f32),
            pltpu.VMEM((4, rows, width), f32),
            dma((3, chunks)), dma((2, 7)), dma((2, 7)),
            dma((chunks, 2)), dma((chunks, 2)), dma((chunks,)), dma((chunks,)),
            dma((3, chunks)), dma((chunks, 2)),
            dma((4,)), dma((4,)), dma((2,)),
        ],
        compiler_params=pltpu.CompilerParams(
            collective_id=0, has_side_effects=True, vmem_limit_bytes=56 * 1024 * 1024
        ),
        cost_estimate=pl.CostEstimate(
            flops=10 * tokens * width * hidden,
            bytes_accessed=6 * width * hidden,
            transcendentals=tokens * hidden,
        ),
    )(activations, out_grad, w_gate, w_up, w_down)


def outer_kernel(act_t_ref, grad_ref, hidden_t_ref, gate_ref, up_ref, gate_out, up_out, down_out):
    tile = 256
    for left, right, out in (
        (act_t_ref, gate_ref, gate_out),
        (act_t_ref, up_ref, up_out),
        (hidden_t_ref, grad_ref, down_out),
    ):
        for n in range(out.shape[1] // tile):
            span = slice(n * tile, (n + 1) * tile)
            out[:, span] = jnp.dot(
                left[...], right[:, span], preferred_element_type=jnp.float32
            ).astype(jnp.bfloat16)


def outer_products(act_t, grad, hidden_t, gate_grad, up_grad):
    width, tokens = act_t.shape
    units = hidden_t.shape[0]
    steps = 8
    down = lambda i: (i, 0)
    whole = lambda i: (0, 0)
    return pl.pallas_call(
        outer_kernel,
        grid=(steps,),
        out_shape=(
            jax.ShapeDtypeStruct((width, units), jnp.bfloat16),
            jax.ShapeDtypeStruct((width, units), jnp.bfloat16),
            jax.ShapeDtypeStruct((units, width), jnp.bfloat16),
        ),
        in_specs=[
            pl.BlockSpec((width // steps, tokens), down),
            pl.BlockSpec((tokens, width), whole),
            pl.BlockSpec((units // steps, tokens), down),
            pl.BlockSpec((tokens, units), whole),
            pl.BlockSpec((tokens, units), whole),
        ],
        out_specs=(
            pl.BlockSpec((width // steps, units), down),
            pl.BlockSpec((width // steps, units), down),
            pl.BlockSpec((units // steps, width), down),
        ),
        compiler_params=pltpu.CompilerParams(vmem_limit_bytes=60 * 1024 * 1024),
        cost_estimate=pl.CostEstimate(
            flops=6 * tokens * width * units,
            bytes_accessed=6 * width * units,
            transcendentals=0,
        ),
    )(act_t, grad, hidden_t, gate_grad, up_grad)


def on_device_fused(activations, out_grad, w_gate, w_up, w_down):
    own, *terms, act_t, grad, hidden_t, gate_grad, up_grad = exchange(
        activations, out_grad, w_gate, w_up, w_down
    )
    for flip, term in zip((2, 4, 6), terms):
        term = lax.ppermute(term, "row", [(i, i ^ flip) for i in range(8)])
        own += term.astype(jnp.float32)
    grad_gate, grad_up, grad_down = outer_products(act_t, grad, hidden_t, gate_grad, up_grad)
    return (own.astype(jnp.bfloat16), grad_gate, grad_up, grad_down)


def solution(mesh):
    placed = (P("row", "col"), P("row", "col"), P("col", "row"), P("col", "row"), P("row", "col"))
    fused = mesh.axis_names == ("row", "col") and dict(mesh.shape) == {"row": 8, "col": 4}
    return jax.shard_map(
        on_device_fused if fused else on_device,
        mesh=mesh,
        in_specs=placed,
        out_specs=(P("row", "col"), P("col", "row"), P("col", "row"), P("row", "col")),
        check_vma=False,
    )
```

```python
import functools

import jax
import jax.numpy as jnp
from jax import lax
from jax.experimental import pallas as pl
from jax.experimental.pallas import tpu as pltpu
from jax.sharding import PartitionSpec as P


def swiglu_parts(summed, width):
    gate = summed[:, :width]
    up_val = summed[:, width : 2 * width]
    hidden_grad = summed[:, 2 * width :]
    sigma = jax.nn.sigmoid(gate)
    hidden = (gate * sigma * up_val).astype(jnp.bfloat16)
    up_grad = (hidden_grad * gate * sigma).astype(jnp.bfloat16)
    gate_grad = (hidden_grad * up_val * sigma * (1.0 + gate * (1.0 - sigma))).astype(jnp.bfloat16)
    return (hidden, gate_grad, up_grad)


def on_device(activations, out_grad, w_gate, w_up, w_down):
    inputs, grads = (
        lax.all_gather(activations, "row", axis=0, tiled=True),
        lax.all_gather(out_grad, "row", axis=0, tiled=True),
    )
    width = w_gate.shape[1]
    contract_last = (((1,), (1,)), ((), ()))
    contract_first = (((0,), (0,)), ((), ()))
    gate_part = jnp.dot(inputs, w_gate, preferred_element_type=jnp.float32)
    up_part = jnp.dot(inputs, w_up, preferred_element_type=jnp.float32)
    back_part = lax.dot_general(grads, w_down, contract_last, preferred_element_type=jnp.float32)
    summed = lax.psum(jnp.concatenate([gate_part, up_part, back_part], axis=1), "col")
    hidden, gate_grad, up_grad = swiglu_parts(summed, width)
    grad_down = lax.dot_general(
        hidden, grads, contract_first, preferred_element_type=jnp.float32
    ).astype(jnp.bfloat16)
    grad_gate = lax.dot_general(
        inputs, gate_grad, contract_first, preferred_element_type=jnp.float32
    ).astype(jnp.bfloat16)
    grad_up = lax.dot_general(
        inputs, up_grad, contract_first, preferred_element_type=jnp.float32
    ).astype(jnp.bfloat16)
    term = lax.dot_general(gate_grad, w_gate, contract_last, preferred_element_type=jnp.float32)
    in_grad = lax.psum_scatter(
        term + lax.dot_general(up_grad, w_up, contract_last, preferred_element_type=jnp.float32),
        "row",
        scatter_dimension=0,
        tiled=True,
    ).astype(jnp.bfloat16)
    return (in_grad, grad_gate, grad_up, grad_down)


MESH = pl.DeviceIdType.MESH
CHUNK = 128
ADD_LAG, PASS_LAG = 2, 4


def nt_dot(a, b):
    return lax.dot_general(a, b, (((1,), (1,)), ((), ())), preferred_element_type=jnp.float32)


def tn_dot(a, b):
    return lax.dot_general(a, b, (((0,), (0,)), ((), ())), preferred_element_type=jnp.float32)


def exchange_kernel(
    act_ref, grad_ref, wg_ref, wu_ref, wd_ref,
    mine_ref, x_ref, y_ref, diag_ref, act_t_hbm, grad_hbm, hidden_t_hbm, gate_hbm, up_hbm,
    both, wgu, wdn, ep, rp, xp, res, own, acc, pair,
    w_sem, gat_send, gat_recv, ep_send, rp_recv, xp_send, xp_recv, res_send, res_recv,
    pair_send, pair_recv, own_sem, out_sem,
    act_t_out, hidden_t_out, gate_out, up_out,
):
    chip_refs = (x_ref, y_ref, diag_ref)
    chunks = wgu.shape[0]
    rows, width = act_ref.shape
    half = rows * 4
    r = lax.axis_index("row")
    c = lax.axis_index("col")
    core = lax.rem(r, 2)
    x = lax.rem(r // 2, 2)
    y = r // 4
    sib = r + 1 - 2 * core
    xn = r + 2 - 4 * x
    yn = r + 4 - 8 * y
    dg = xn + 4 - 8 * y
    last = chunks - 1

    def weight_copies(j):
        cols = pl.ds(pl.multiple_of(j * CHUNK, CHUNK), CHUNK)
        return (
            pltpu.make_async_copy(wg_ref.at[:, cols], wgu.at[j, :, pl.ds(0, CHUNK)], w_sem.at[0, j]),
            pltpu.make_async_copy(wu_ref.at[:, cols], wgu.at[j, :, pl.ds(CHUNK, CHUNK)], w_sem.at[1, j]),
            pltpu.make_async_copy(wd_ref.at[cols, :], wdn.at[j], w_sem.at[2, j]),
        )

    def start_weights(j, carry):
        for copy in weight_copies(j):
            copy.start()
        return carry

    barrier = pltpu.get_barrier_semaphore()
    for other in (sib, xn, yn, dg):
        pl.semaphore_signal(barrier, inc=1, device_id=(other, c), device_id_type=MESH)

    @pl.when(c > 0)
    def _():
        pl.semaphore_signal(barrier, inc=1, device_id=(r, c - 1), device_id_type=MESH)

    @pl.when(c < 3)
    def _():
        pl.semaphore_signal(barrier, inc=1, device_id=(r, c + 1), device_id_type=MESH)

    lax.fori_loop(0, chunks, start_weights, 0)
    mine = pl.ds(pl.multiple_of(r * rows, rows), rows)
    locals_ = (
        pltpu.make_async_copy(act_ref, both.at[0, mine], own_sem.at[0]),
        pltpu.make_async_copy(grad_ref, both.at[1, mine], own_sem.at[1]),
    )
    for copy in locals_:
        copy.start()
    acc[...] = jnp.zeros_like(acc)

    end = (c == 0) | (c == 3)

    @pl.when(end)
    def _():
        pl.semaphore_wait(barrier, 5)

    @pl.when(jnp.logical_not(end))
    def _():
        pl.semaphore_wait(barrier, 6)

    def block(a, index):
        return both.at[a, pl.ds(pl.multiple_of(index * rows, rows), rows)]

    def gather(a, index, to, kind):
        return pltpu.make_async_remote_copy(
            src_ref=(act_ref, grad_ref)[a] if index is r else block(a, index), dst_ref=block(a, index),
            send_sem=gat_send.at[a, kind], recv_sem=gat_recv.at[a, kind],
            device_id=(to, c), device_id_type=MESH,
        )

    sent = []
    for a in (0, 1):
        sent += [gather(a, r, xn, 0), gather(a, r, yn, 1), gather(a, r, sib, 3)]
    for copy in sent:
        copy.start()
    gather(0, xn, xn, 0).wait_recv()
    sent.append(gather(0, xn, yn, 2))
    sent[-1].start()
    gather(1, yn, yn, 1).wait_recv()
    sent.append(gather(1, yn, xn, 2))
    sent[-1].start()
    for a, index, kind in ((0, xn, 4), (1, yn, 5)):
        sent.append(gather(a, index, sib, kind))
        sent[-1].start()
    gather(0, yn, yn, 1).wait_recv()
    gather(1, xn, xn, 0).wait_recv()
    for a, index, kind in ((0, yn, 5), (1, xn, 4)):
        sent.append(gather(a, index, sib, kind))
        sent[-1].start()
    for a in (0, 1):
        gather(a, dg, yn, 2).wait_recv()
        sent.append(gather(a, dg, sib, 6))
        sent[-1].start()
    for a in (0, 1):
        for kind, index in ((3, r), (4, xn), (5, yn), (6, dg)):
            gather(a, index + sib - r, sib, kind).wait_recv()

    for copy in locals_:
        copy.wait()
    grad_copy = pltpu.make_async_copy(both.at[1], grad_hbm, out_sem.at[0])
    grad_copy.start()

    inner = jnp.where(c == 0, 1, 2)
    outer = jnp.where(c == 1, 0, 3)
    peer = 3 - c
    mine_h = jnp.where(c == 2, 1, 0)
    other_h = 1 - mine_h
    first_h = jnp.where(c == 0, 1, 0)

    def to_inner(j, h):
        return pltpu.make_async_remote_copy(
            src_ref=ep.at[j, h], dst_ref=rp.at[j, h], send_sem=ep_send.at[j, h], recv_sem=rp_recv.at[j, h],
            device_id=(r, inner), device_id_type=MESH,
        )

    def from_outer(j, h):
        return pltpu.make_async_remote_copy(
            src_ref=ep.at[j, h], dst_ref=rp.at[j, h], send_sem=ep_send.at[j, h], recv_sem=rp_recv.at[j, h],
            device_id=(r, outer), device_id_type=MESH,
        )

    def to_peer(j):
        return pltpu.make_async_remote_copy(
            src_ref=ep.at[j, other_h], dst_ref=xp.at[j], send_sem=xp_send.at[j], recv_sem=xp_recv.at[j],
            device_id=(r, peer), device_id_type=MESH,
        )

    def result(j, h, to, kind):
        return pltpu.make_async_remote_copy(
            src_ref=res.at[j, h], dst_ref=res.at[j, h], send_sem=res_send.at[kind, j], recv_sem=res_recv.at[j, h],
            device_id=(r, to), device_id_type=MESH,
        )

    def part(j):
        for copy in weight_copies(j):
            copy.wait()
        front = jnp.dot(both[0], wgu[j], preferred_element_type=jnp.float32)
        back = nt_dot(both[1], wdn[j])
        return jnp.concatenate([front, back], axis=1)

    def finish(j):
        cols = pl.ds(pl.multiple_of(j * CHUNK, CHUNK), CHUNK)
        ready = res[j].reshape(2 * half, 3 * CHUNK)
        hidden_t_out[cols, :] = ready[:, :CHUNK].T
        gate_out[:, cols] = ready[:, CHUNK : 2 * CHUNK]
        up_out[:, cols] = ready[:, 2 * CHUNK :]
        for n in range(4):
            span = slice(n * width // 4, (n + 1) * width // 4)
            acc[:, span] += nt_dot(ready[:, CHUNK:], wgu[j, span, :])

        @pl.when(j < 8)
        def _():
            span = pl.ds(pl.multiple_of(j * (width // 8), width // 8), width // 8)
            act_t_out[span, :] = both[0, :, span].T

    @pl.when(end)
    def _():
        def send(j, carry):
            total = part(j)
            ep[j] = total.astype(jnp.bfloat16).reshape(2, half, 3 * CHUNK)
            to_inner(j, first_h).start()
            to_inner(j, 1 - first_h).start()
            return carry

        def take(j, carry):
            for h in (0, 1):
                result(j, h, inner, 0).wait_recv()
            finish(j)
            return carry

        def drain(j, carry):
            for h in (0, 1):
                to_inner(j, h).wait_send()
            return carry

        lax.fori_loop(0, chunks, send, 0)
        lax.fori_loop(0, chunks, take, 0)
        lax.fori_loop(0, chunks, drain, 0)

    @pl.when(jnp.logical_not(end))
    def _():
        def step(i, carry):
            @pl.when(i <= last)
            def _():
                own[lax.rem(i, 4)] = part(i).reshape(2, half, 3 * CHUNK)
                from_outer(i, other_h).wait_recv()
                ep[i, other_h] = (
                    own[lax.rem(i, 4), other_h] + rp[i, other_h].astype(jnp.float32)
                ).astype(jnp.bfloat16)
                to_peer(i).start()

            @pl.when((i >= ADD_LAG) & (i < chunks + ADD_LAG))
            def _():
                j = i - ADD_LAG
                from_outer(j, mine_h).wait_recv()
                to_peer(j).wait_recv()
                total = own[lax.rem(j, 4), mine_h] + (
                    rp[j, mine_h].astype(jnp.float32) + xp[j].astype(jnp.float32)
                )
                res[j, mine_h] = jnp.concatenate(swiglu_parts(total, CHUNK), axis=1)
                result(j, mine_h, peer, 0).start()
                result(j, mine_h, outer, 1).start()

            @pl.when(i >= PASS_LAG)
            def _():
                j = i - PASS_LAG
                result(j, other_h, peer, 0).wait_recv()
                result(j, other_h, outer, 2).start()
                finish(j)

            return carry

        def drain(j, carry):
            to_peer(j).wait_send()
            result(j, mine_h, peer, 0).wait_send()
            result(j, mine_h, outer, 1).wait_send()
            result(j, other_h, outer, 2).wait_send()
            return carry

        lax.fori_loop(0, chunks + PASS_LAG, step, 0)
        lax.fori_loop(0, chunks, drain, 0)

    outs = [grad_copy] + [
        pltpu.make_async_copy(src, dst, out_sem.at[k + 1])
        for k, (src, dst) in enumerate(
            ((act_t_out, act_t_hbm), (hidden_t_out, hidden_t_hbm), (gate_out, gate_hbm), (up_out, up_hbm))
        )
    ]

    def term(index):
        return pl.ds(pl.multiple_of(index * rows, rows), rows)

    def to_sib(k):
        return pltpu.make_async_remote_copy(
            src_ref=acc.at[term(2 * k + 1 - core)], dst_ref=pair.at[k],
            send_sem=pair_send.at[k], recv_sem=pair_recv.at[k],
            device_id=(sib, c), device_id_type=MESH,
        )

    for k in range(4):
        to_sib(k).start()
    for copy in outs[1:]:
        copy.start()
    for copy in sent:
        copy.wait_send()
    for k in range(4):
        to_sib(k).wait_recv()

    def summed(index):
        return acc[term(index)] + pair[index // 2]

    mine_ref[...] = summed(r)
    for kind, to in enumerate((xn, yn, dg)):
        chip_refs[kind][...] = summed(to).astype(jnp.bfloat16)
    for k in range(4):
        to_sib(k).wait_send()
    for copy in outs:
        copy.wait()


def exchange(activations, out_grad, w_gate, w_up, w_down):
    rows, width = activations.shape
    hidden = w_gate.shape[1]
    tokens, chunks, half = 8 * rows, hidden // CHUNK, 4 * rows
    vmem = pl.BlockSpec(memory_space=pltpu.VMEM)
    anywhere = pl.BlockSpec(memory_space=pl.ANY)
    bf16, f32, dma = jnp.bfloat16, jnp.float32, pltpu.SemaphoreType.DMA
    return pl.pallas_call(
        exchange_kernel,
        out_shape=(
            jax.ShapeDtypeStruct((rows, width), f32),
            jax.ShapeDtypeStruct((rows, width), bf16),
            jax.ShapeDtypeStruct((rows, width), bf16),
            jax.ShapeDtypeStruct((rows, width), bf16),
            jax.ShapeDtypeStruct((width, tokens), bf16),
            jax.ShapeDtypeStruct((tokens, width), bf16),
            jax.ShapeDtypeStruct((hidden, tokens), bf16),
            jax.ShapeDtypeStruct((tokens, hidden), bf16),
            jax.ShapeDtypeStruct((tokens, hidden), bf16),
        ),
        in_specs=[vmem, vmem, anywhere, anywhere, anywhere],
        out_specs=(vmem,) * 4 + (anywhere,) * 5,
        scratch_shapes=[
            pltpu.VMEM((2, tokens, width), bf16),
            pltpu.VMEM((chunks, width, 2 * CHUNK), bf16),
            pltpu.VMEM((chunks, CHUNK, width), bf16),
            pltpu.VMEM((chunks, 2, half, 3 * CHUNK), bf16),
            pltpu.VMEM((chunks, 2, half, 3 * CHUNK), bf16),
            pltpu.VMEM((chunks, half, 3 * CHUNK), bf16),
            pltpu.VMEM((chunks, 2, half, 3 * CHUNK), bf16),
            pltpu.VMEM((4, 2, half, 3 * CHUNK), f32),
            pltpu.VMEM((tokens, width), f32),
            pltpu.VMEM((4, rows, width), f32),
            dma((3, chunks)), dma((2, 7)), dma((2, 7)),
            dma((chunks, 2)), dma((chunks, 2)), dma((chunks,)), dma((chunks,)),
            dma((3, chunks)), dma((chunks, 2)),
            dma((4,)), dma((4,)), dma((2,)), dma((5,)),
            pltpu.VMEM((width, tokens), bf16),
            pltpu.VMEM((hidden, tokens), bf16),
            pltpu.VMEM((tokens, hidden), bf16),
            pltpu.VMEM((tokens, hidden), bf16),
        ],
        compiler_params=pltpu.CompilerParams(
            collective_id=0, has_side_effects=True, vmem_limit_bytes=56 * 1024 * 1024
        ),
        cost_estimate=pl.CostEstimate(
            flops=10 * tokens * width * hidden,
            bytes_accessed=6 * width * hidden,
            transcendentals=tokens * hidden,
        ),
    )(activations, out_grad, w_gate, w_up, w_down)


def outer_kernel(act_t_ref, grad_ref, hidden_t_ref, gate_ref, up_ref, gate_out, up_out, down_out):
    tile = 256
    for left, right, out in (
        (act_t_ref, gate_ref, gate_out),
        (act_t_ref, up_ref, up_out),
        (hidden_t_ref, grad_ref, down_out),
    ):
        for n in range(out.shape[1] // tile):
            span = slice(n * tile, (n + 1) * tile)
            out[:, span] = jnp.dot(
                left[...], right[:, span], preferred_element_type=jnp.float32
            ).astype(jnp.bfloat16)


def outer_products(act_t, grad, hidden_t, gate_grad, up_grad):
    width, tokens = act_t.shape
    units = hidden_t.shape[0]
    steps = 8
    down = lambda i: (i, 0)
    whole = lambda i: (0, 0)
    return pl.pallas_call(
        outer_kernel,
        grid=(steps,),
        out_shape=(
            jax.ShapeDtypeStruct((width, units), jnp.bfloat16),
            jax.ShapeDtypeStruct((width, units), jnp.bfloat16),
            jax.ShapeDtypeStruct((units, width), jnp.bfloat16),
        ),
        in_specs=[
            pl.BlockSpec((width // steps, tokens), down),
            pl.BlockSpec((tokens, width), whole),
            pl.BlockSpec((units // steps, tokens), down),
            pl.BlockSpec((tokens, units), whole),
            pl.BlockSpec((tokens, units), whole),
        ],
        out_specs=(
            pl.BlockSpec((width // steps, units), down),
            pl.BlockSpec((width // steps, units), down),
            pl.BlockSpec((units // steps, width), down),
        ),
        compiler_params=pltpu.CompilerParams(vmem_limit_bytes=60 * 1024 * 1024),
        cost_estimate=pl.CostEstimate(
            flops=6 * tokens * width * units,
            bytes_accessed=6 * width * units,
            transcendentals=0,
        ),
    )(act_t, grad, hidden_t, gate_grad, up_grad)


def on_device_fused(activations, out_grad, w_gate, w_up, w_down):
    own, *terms, act_t, grad, hidden_t, gate_grad, up_grad = exchange(
        activations, out_grad, w_gate, w_up, w_down
    )
    for flip, term in zip((2, 4, 6), terms):
        term = lax.ppermute(term, "row", [(i, i ^ flip) for i in range(8)])
        own += term.astype(jnp.float32)
    grad_gate, grad_up, grad_down = outer_products(act_t, grad, hidden_t, gate_grad, up_grad)
    return (own.astype(jnp.bfloat16), grad_gate, grad_up, grad_down)


def solution(mesh):
    placed = (P("row", "col"), P("row", "col"), P("col", "row"), P("col", "row"), P("row", "col"))
    fused = mesh.axis_names == ("row", "col") and dict(mesh.shape) == {"row": 8, "col": 4}
    return jax.shard_map(
        on_device_fused if fused else on_device,
        mesh=mesh,
        in_specs=placed,
        out_specs=(P("row", "col"), P("col", "row"), P("col", "row"), P("row", "col")),
        check_vma=False,
    )
```

```python
import functools

import jax
import jax.numpy as jnp
from jax import lax
from jax.experimental import pallas as pl
from jax.experimental.pallas import tpu as pltpu
from jax.sharding import PartitionSpec as P


def swiglu_parts(summed, width):
    gate = summed[:, :width]
    up_val = summed[:, width : 2 * width]
    hidden_grad = summed[:, 2 * width :]
    sigma = jax.nn.sigmoid(gate)
    hidden = (gate * sigma * up_val).astype(jnp.bfloat16)
    up_grad = (hidden_grad * gate * sigma).astype(jnp.bfloat16)
    gate_grad = (hidden_grad * up_val * sigma * (1.0 + gate * (1.0 - sigma))).astype(jnp.bfloat16)
    return (hidden, gate_grad, up_grad)


def on_device(activations, out_grad, w_gate, w_up, w_down):
    inputs, grads = (
        lax.all_gather(activations, "row", axis=0, tiled=True),
        lax.all_gather(out_grad, "row", axis=0, tiled=True),
    )
    width = w_gate.shape[1]
    contract_last = (((1,), (1,)), ((), ()))
    contract_first = (((0,), (0,)), ((), ()))
    gate_part = jnp.dot(inputs, w_gate, preferred_element_type=jnp.float32)
    up_part = jnp.dot(inputs, w_up, preferred_element_type=jnp.float32)
    back_part = lax.dot_general(grads, w_down, contract_last, preferred_element_type=jnp.float32)
    summed = lax.psum(jnp.concatenate([gate_part, up_part, back_part], axis=1), "col")
    hidden, gate_grad, up_grad = swiglu_parts(summed, width)
    grad_down = lax.dot_general(
        hidden, grads, contract_first, preferred_element_type=jnp.float32
    ).astype(jnp.bfloat16)
    grad_gate = lax.dot_general(
        inputs, gate_grad, contract_first, preferred_element_type=jnp.float32
    ).astype(jnp.bfloat16)
    grad_up = lax.dot_general(
        inputs, up_grad, contract_first, preferred_element_type=jnp.float32
    ).astype(jnp.bfloat16)
    term = lax.dot_general(gate_grad, w_gate, contract_last, preferred_element_type=jnp.float32)
    in_grad = lax.psum_scatter(
        term + lax.dot_general(up_grad, w_up, contract_last, preferred_element_type=jnp.float32),
        "row",
        scatter_dimension=0,
        tiled=True,
    ).astype(jnp.bfloat16)
    return (in_grad, grad_gate, grad_up, grad_down)


MESH = pl.DeviceIdType.MESH
CHUNK = 128
ADD_LAG, PASS_LAG = 3, 6


def nt_dot(a, b):
    return lax.dot_general(a, b, (((1,), (1,)), ((), ())), preferred_element_type=jnp.float32)


def tn_dot(a, b):
    return lax.dot_general(a, b, (((0,), (0,)), ((), ())), preferred_element_type=jnp.float32)


def exchange_kernel(
    act_ref, grad_ref, wg_ref, wu_ref, wd_ref,
    mine_ref, x_ref, y_ref, diag_ref, act_t_hbm, grad_hbm, hidden_t_hbm, gate_hbm, up_hbm,
    both, wgu, wdn, ep, rp, xp, res, own, acc, pair,
    w_sem, gat_send, gat_recv, ep_send, rp_recv, xp_send, xp_recv, res_send, res_recv,
    pair_send, pair_recv, own_sem, out_sem,
    act_t_out, hidden_t_out, gate_out, up_out,
):
    chip_refs = (x_ref, y_ref, diag_ref)
    chunks = wgu.shape[0]
    rows, width = act_ref.shape
    half = rows * 4
    r = lax.axis_index("row")
    c = lax.axis_index("col")
    core = lax.rem(r, 2)
    x = lax.rem(r // 2, 2)
    y = r // 4
    sib = r + 1 - 2 * core
    xn = r + 2 - 4 * x
    yn = r + 4 - 8 * y
    dg = xn + 4 - 8 * y
    last = chunks - 1

    def weight_copies(j):
        cols = pl.ds(pl.multiple_of(j * CHUNK, CHUNK), CHUNK)
        return (
            pltpu.make_async_copy(wg_ref.at[:, cols], wgu.at[j, :, pl.ds(0, CHUNK)], w_sem.at[0, j]),
            pltpu.make_async_copy(wu_ref.at[:, cols], wgu.at[j, :, pl.ds(CHUNK, CHUNK)], w_sem.at[1, j]),
            pltpu.make_async_copy(wd_ref.at[cols, :], wdn.at[j], w_sem.at[2, j]),
        )

    def start_weights(j, carry):
        for copy in weight_copies(j):
            copy.start()
        return carry

    barrier = pltpu.get_barrier_semaphore()
    for other in (sib, xn, yn, dg):
        pl.semaphore_signal(barrier, inc=1, device_id=(other, c), device_id_type=MESH)

    @pl.when(c > 0)
    def _():
        pl.semaphore_signal(barrier, inc=1, device_id=(r, c - 1), device_id_type=MESH)

    @pl.when(c < 3)
    def _():
        pl.semaphore_signal(barrier, inc=1, device_id=(r, c + 1), device_id_type=MESH)

    lax.fori_loop(0, chunks, start_weights, 0)
    mine = pl.ds(pl.multiple_of(r * rows, rows), rows)
    locals_ = (
        pltpu.make_async_copy(act_ref, both.at[0, mine], own_sem.at[0]),
        pltpu.make_async_copy(grad_ref, both.at[1, mine], own_sem.at[1]),
    )
    for copy in locals_:
        copy.start()
    acc[...] = jnp.zeros_like(acc)

    end = (c == 0) | (c == 3)

    @pl.when(end)
    def _():
        pl.semaphore_wait(barrier, 5)

    @pl.when(jnp.logical_not(end))
    def _():
        pl.semaphore_wait(barrier, 6)

    def block(a, index):
        return both.at[a, pl.ds(pl.multiple_of(index * rows, rows), rows)]

    def gather(a, index, to, kind):
        return pltpu.make_async_remote_copy(
            src_ref=(act_ref, grad_ref)[a] if index is r else block(a, index), dst_ref=block(a, index),
            send_sem=gat_send.at[a, kind], recv_sem=gat_recv.at[a, kind],
            device_id=(to, c), device_id_type=MESH,
        )

    sent = []
    for a in (0, 1):
        sent += [gather(a, r, xn, 0), gather(a, r, yn, 1), gather(a, r, sib, 3)]
    for copy in sent:
        copy.start()
    gather(0, xn, xn, 0).wait_recv()
    sent.append(gather(0, xn, yn, 2))
    sent[-1].start()
    gather(1, yn, yn, 1).wait_recv()
    sent.append(gather(1, yn, xn, 2))
    sent[-1].start()
    for a, index, kind in ((0, xn, 4), (1, yn, 5)):
        sent.append(gather(a, index, sib, kind))
        sent[-1].start()
    gather(0, yn, yn, 1).wait_recv()
    gather(1, xn, xn, 0).wait_recv()
    for a, index, kind in ((0, yn, 5), (1, xn, 4)):
        sent.append(gather(a, index, sib, kind))
        sent[-1].start()
    for a in (0, 1):
        gather(a, dg, yn, 2).wait_recv()
        sent.append(gather(a, dg, sib, 6))
        sent[-1].start()
    for a in (0, 1):
        for kind, index in ((3, r), (4, xn), (5, yn), (6, dg)):
            gather(a, index + sib - r, sib, kind).wait_recv()

    for copy in locals_:
        copy.wait()
    grad_copy = pltpu.make_async_copy(both.at[1], grad_hbm, out_sem.at[0])
    grad_copy.start()

    inner = jnp.where(c == 0, 1, 2)
    outer = jnp.where(c == 1, 0, 3)
    peer = 3 - c
    mine_h = jnp.where(c == 2, 1, 0)
    other_h = 1 - mine_h
    first_h = jnp.where(c == 0, 1, 0)

    def to_inner(j, h):
        return pltpu.make_async_remote_copy(
            src_ref=ep.at[j, h], dst_ref=rp.at[j, h], send_sem=ep_send.at[j, h], recv_sem=rp_recv.at[j, h],
            device_id=(r, inner), device_id_type=MESH,
        )

    def from_outer(j, h):
        return pltpu.make_async_remote_copy(
            src_ref=ep.at[j, h], dst_ref=rp.at[j, h], send_sem=ep_send.at[j, h], recv_sem=rp_recv.at[j, h],
            device_id=(r, outer), device_id_type=MESH,
        )

    def to_peer(j):
        return pltpu.make_async_remote_copy(
            src_ref=ep.at[j, other_h], dst_ref=xp.at[j], send_sem=xp_send.at[j], recv_sem=xp_recv.at[j],
            device_id=(r, peer), device_id_type=MESH,
        )

    def result(j, h, to, kind):
        return pltpu.make_async_remote_copy(
            src_ref=res.at[j, h], dst_ref=res.at[j, h], send_sem=res_send.at[kind, j], recv_sem=res_recv.at[j, h],
            device_id=(r, to), device_id_type=MESH,
        )

    def part(j):
        for copy in weight_copies(j):
            copy.wait()
        front = jnp.dot(both[0], wgu[j], preferred_element_type=jnp.float32)
        back = nt_dot(both[1], wdn[j])
        return jnp.concatenate([front, back], axis=1)

    def finish(j):
        cols = pl.ds(pl.multiple_of(j * CHUNK, CHUNK), CHUNK)
        ready = res[j].reshape(2 * half, 3 * CHUNK)
        hidden_t_out[cols, :] = ready[:, :CHUNK].T
        gate_out[:, cols] = ready[:, CHUNK : 2 * CHUNK]
        up_out[:, cols] = ready[:, 2 * CHUNK :]
        for n in range(4):
            span = slice(n * width // 4, (n + 1) * width // 4)
            acc[:, span] += nt_dot(ready[:, CHUNK:], wgu[j, span, :])

        @pl.when(j < 8)
        def _():
            span = pl.ds(pl.multiple_of(j * (width // 8), width // 8), width // 8)
            act_t_out[span, :] = both[0, :, span].T

    @pl.when(end)
    def _():
        def send(j, carry):
            total = part(j)
            ep[j] = total.astype(jnp.bfloat16).reshape(2, half, 3 * CHUNK)
            to_inner(j, first_h).start()
            to_inner(j, 1 - first_h).start()
            return carry

        def take(j, carry):
            for h in (0, 1):
                result(j, h, inner, 0).wait_recv()
            finish(j)
            return carry

        def drain(j, carry):
            for h in (0, 1):
                to_inner(j, h).wait_send()
            return carry

        lax.fori_loop(0, chunks, send, 0)
        lax.fori_loop(0, chunks, take, 0)
        lax.fori_loop(0, chunks, drain, 0)

    @pl.when(jnp.logical_not(end))
    def _():
        def step(i, carry):
            @pl.when(i <= last)
            def _():
                own[lax.rem(i, 4)] = part(i).reshape(2, half, 3 * CHUNK)
                from_outer(i, other_h).wait_recv()
                ep[i, other_h] = (
                    own[lax.rem(i, 4), other_h] + rp[i, other_h].astype(jnp.float32)
                ).astype(jnp.bfloat16)
                to_peer(i).start()

            @pl.when((i >= ADD_LAG) & (i < chunks + ADD_LAG))
            def _():
                j = i - ADD_LAG
                from_outer(j, mine_h).wait_recv()
                to_peer(j).wait_recv()
                total = own[lax.rem(j, 4), mine_h] + (
                    rp[j, mine_h].astype(jnp.float32) + xp[j].astype(jnp.float32)
                )
                res[j, mine_h] = jnp.concatenate(swiglu_parts(total, CHUNK), axis=1)
                result(j, mine_h, peer, 0).start()
                result(j, mine_h, outer, 1).start()

            @pl.when(i >= PASS_LAG)
            def _():
                j = i - PASS_LAG
                result(j, other_h, peer, 0).wait_recv()
                result(j, other_h, outer, 2).start()
                finish(j)

            return carry

        def drain(j, carry):
            to_peer(j).wait_send()
            result(j, mine_h, peer, 0).wait_send()
            result(j, mine_h, outer, 1).wait_send()
            result(j, other_h, outer, 2).wait_send()
            return carry

        lax.fori_loop(0, chunks + PASS_LAG, step, 0)
        lax.fori_loop(0, chunks, drain, 0)

    outs = [grad_copy] + [
        pltpu.make_async_copy(src, dst, out_sem.at[k + 1])
        for k, (src, dst) in enumerate(
            ((act_t_out, act_t_hbm), (hidden_t_out, hidden_t_hbm), (gate_out, gate_hbm), (up_out, up_hbm))
        )
    ]

    def term(index):
        return pl.ds(pl.multiple_of(index * rows, rows), rows)

    def to_sib(k):
        return pltpu.make_async_remote_copy(
            src_ref=acc.at[term(2 * k + 1 - core)], dst_ref=pair.at[k],
            send_sem=pair_send.at[k], recv_sem=pair_recv.at[k],
            device_id=(sib, c), device_id_type=MESH,
        )

    for k in range(4):
        to_sib(k).start()
    for copy in outs[1:]:
        copy.start()
    for copy in sent:
        copy.wait_send()
    for k in range(4):
        to_sib(k).wait_recv()

    def summed(index):
        return acc[term(index)] + pair[index // 2]

    mine_ref[...] = summed(r)
    for kind, to in enumerate((xn, yn, dg)):
        chip_refs[kind][...] = summed(to).astype(jnp.bfloat16)
    for k in range(4):
        to_sib(k).wait_send()
    for copy in outs:
        copy.wait()


def exchange(activations, out_grad, w_gate, w_up, w_down):
    rows, width = activations.shape
    hidden = w_gate.shape[1]
    tokens, chunks, half = 8 * rows, hidden // CHUNK, 4 * rows
    vmem = pl.BlockSpec(memory_space=pltpu.VMEM)
    anywhere = pl.BlockSpec(memory_space=pl.ANY)
    bf16, f32, dma = jnp.bfloat16, jnp.float32, pltpu.SemaphoreType.DMA
    return pl.pallas_call(
        exchange_kernel,
        out_shape=(
            jax.ShapeDtypeStruct((rows, width), f32),
            jax.ShapeDtypeStruct((rows, width), bf16),
            jax.ShapeDtypeStruct((rows, width), bf16),
            jax.ShapeDtypeStruct((rows, width), bf16),
            jax.ShapeDtypeStruct((width, tokens), bf16),
            jax.ShapeDtypeStruct((tokens, width), bf16),
            jax.ShapeDtypeStruct((hidden, tokens), bf16),
            jax.ShapeDtypeStruct((tokens, hidden), bf16),
            jax.ShapeDtypeStruct((tokens, hidden), bf16),
        ),
        in_specs=[vmem, vmem, anywhere, anywhere, anywhere],
        out_specs=(vmem,) * 4 + (anywhere,) * 5,
        scratch_shapes=[
            pltpu.VMEM((2, tokens, width), bf16),
            pltpu.VMEM((chunks, width, 2 * CHUNK), bf16),
            pltpu.VMEM((chunks, CHUNK, width), bf16),
            pltpu.VMEM((chunks, 2, half, 3 * CHUNK), bf16),
            pltpu.VMEM((chunks, 2, half, 3 * CHUNK), bf16),
            pltpu.VMEM((chunks, half, 3 * CHUNK), bf16),
            pltpu.VMEM((chunks, 2, half, 3 * CHUNK), bf16),
            pltpu.VMEM((4, 2, half, 3 * CHUNK), f32),
            pltpu.VMEM((tokens, width), f32),
            pltpu.VMEM((4, rows, width), f32),
            dma((3, chunks)), dma((2, 7)), dma((2, 7)),
            dma((chunks, 2)), dma((chunks, 2)), dma((chunks,)), dma((chunks,)),
            dma((3, chunks)), dma((chunks, 2)),
            dma((4,)), dma((4,)), dma((2,)), dma((5,)),
            pltpu.VMEM((width, tokens), bf16),
            pltpu.VMEM((hidden, tokens), bf16),
            pltpu.VMEM((tokens, hidden), bf16),
            pltpu.VMEM((tokens, hidden), bf16),
        ],
        compiler_params=pltpu.CompilerParams(
            collective_id=0, has_side_effects=True, vmem_limit_bytes=56 * 1024 * 1024
        ),
        cost_estimate=pl.CostEstimate(
            flops=10 * tokens * width * hidden,
            bytes_accessed=6 * width * hidden,
            transcendentals=tokens * hidden,
        ),
    )(activations, out_grad, w_gate, w_up, w_down)


def outer_kernel(act_t_ref, grad_ref, hidden_t_ref, gate_ref, up_ref, gate_out, up_out, down_out):
    tile = 256
    for left, right, out in (
        (act_t_ref, gate_ref, gate_out),
        (act_t_ref, up_ref, up_out),
        (hidden_t_ref, grad_ref, down_out),
    ):
        for n in range(out.shape[1] // tile):
            span = slice(n * tile, (n + 1) * tile)
            out[:, span] = jnp.dot(
                left[...], right[:, span], preferred_element_type=jnp.float32
            ).astype(jnp.bfloat16)


def outer_products(act_t, grad, hidden_t, gate_grad, up_grad):
    width, tokens = act_t.shape
    units = hidden_t.shape[0]
    steps = 8
    down = lambda i: (i, 0)
    whole = lambda i: (0, 0)
    return pl.pallas_call(
        outer_kernel,
        grid=(steps,),
        out_shape=(
            jax.ShapeDtypeStruct((width, units), jnp.bfloat16),
            jax.ShapeDtypeStruct((width, units), jnp.bfloat16),
            jax.ShapeDtypeStruct((units, width), jnp.bfloat16),
        ),
        in_specs=[
            pl.BlockSpec((width // steps, tokens), down),
            pl.BlockSpec((tokens, width), whole),
            pl.BlockSpec((units // steps, tokens), down),
            pl.BlockSpec((tokens, units), whole),
            pl.BlockSpec((tokens, units), whole),
        ],
        out_specs=(
            pl.BlockSpec((width // steps, units), down),
            pl.BlockSpec((width // steps, units), down),
            pl.BlockSpec((units // steps, width), down),
        ),
        compiler_params=pltpu.CompilerParams(vmem_limit_bytes=60 * 1024 * 1024),
        cost_estimate=pl.CostEstimate(
            flops=6 * tokens * width * units,
            bytes_accessed=6 * width * units,
            transcendentals=0,
        ),
    )(act_t, grad, hidden_t, gate_grad, up_grad)


def on_device_fused(activations, out_grad, w_gate, w_up, w_down):
    own, *terms, act_t, grad, hidden_t, gate_grad, up_grad = exchange(
        activations, out_grad, w_gate, w_up, w_down
    )
    for flip, term in zip((2, 4, 6), terms):
        term = lax.ppermute(term, "row", [(i, i ^ flip) for i in range(8)])
        own += term.astype(jnp.float32)
    grad_gate, grad_up, grad_down = outer_products(act_t, grad, hidden_t, gate_grad, up_grad)
    return (own.astype(jnp.bfloat16), grad_gate, grad_up, grad_down)


def solution(mesh):
    placed = (P("row", "col"), P("row", "col"), P("col", "row"), P("col", "row"), P("row", "col"))
    fused = mesh.axis_names == ("row", "col") and dict(mesh.shape) == {"row": 8, "col": 4}
    return jax.shard_map(
        on_device_fused if fused else on_device,
        mesh=mesh,
        in_specs=placed,
        out_specs=(P("row", "col"), P("col", "row"), P("col", "row"), P("row", "col")),
        check_vma=False,
    )
```
